256 devices in a mesh: dom: 16 (over x, y), row: 8 (over z), rep: 2 (over core).
Axes of the slice: x: 4, y: 4, z: 8, core: 2. Of those that a mesh axis runs over, the one named last changes fastest.
Arguments:
- features: float32 [65536, 128], P(('dom', 'row', 'rep')), may hold values from -6 to 6
- send_rows: int32 [16, 8, 16, 128], P('dom', 'row'), may hold values from 0 to 511
- tile_values: float32 [16, 8, 128, 128, 128], P('dom', 'row', 'rep'), may hold values from -0.125 to 0.125
- tile_rows: int32 [16, 8, 128], P('dom', 'row', 'rep'), may hold values from 0 to 3
- tile_cols: int32 [16, 8, 128], P('dom', 'row', 'rep'), may hold values from 0 to 47
- tile_counts: int32 [16, 8, 2], P('dom', 'row', 'rep'), may hold values from 1 to 64, as said below
- history: float32 [262144, 256], P(('dom', 'row')), may hold values from -4 to 4
- weight_one: float32 [128, 256], replicated, may hold values from -0.5 to 0.5
- weight_two: float32 [256, 256], replicated, may hold values from -0.375 to 0.375
- cotangent: float32 [65536, 256], P(('dom', 'row')), may hold values from -0.0234375 to 0.0234375
Outputs:
- output: float32 [65536, 256], P(('dom', 'row', 'rep'))
- grad_one: float32 [128, 256], replicated
- grad_two: float32 [256, 256], replicated
- fresh_halo: float32 [262144, 256], P(('dom', 'row'))
The draws below stay inside these ranges and needn't reach their ends.
Inputs may be any that keep to these rules, and one draw needn't show every extreme that they name: `send_rows`: each entry names a node of the sending panel; entries may repeat. `tile_counts`: some device has all 64 slots live.
All inputs are finite; a program needn't handle non-finite values.
Results may differ from the reference program's by a relative error of at most 0.0003.
Values sent between devices are 32-bit elements; how exact they have to be, the bound alone decides.
No kernel may reach another device: no remote copies, remote signals or barrier semaphores. Data moves between devices by JAX's collectives and lax.ppermute only.
A program may use at most 128 MiB of HBM per device.

```python
import jax
import jax.numpy as jnp
from jax import lax

F = 128
H = 256
TILE = 128
BLK_DEV = 4
TILES_DEV = 64
TILES = 128
PANEL = 512
NODES = 65536
COLS = 48
N_DOM = 16
N_ROW = 8
N_REP = 2


def draw_tile_counts(key, part):
    key = jax.random.fold_in(key, 11)
    first_key, second_key, third_key = jax.random.split(key, 3)
    count_shape = (N_DOM, N_ROW, N_REP)
    base_counts = jax.random.randint(first_key, count_shape, max(TILES_DEV // 8, 1), TILES_DEV // 2 + 1)
    full_marks = jax.random.randint(second_key, count_shape, 0, 8) == 0
    chosen = jax.random.randint(third_key, (), 0, N_DOM * N_ROW * N_REP)
    flat_index = jnp.arange(N_DOM * N_ROW * N_REP, dtype=jnp.int32).reshape(count_shape)
    full_marks = full_marks | (flat_index == chosen)
    return jnp.where(full_marks, TILES_DEV, base_counts).astype(jnp.int32)


def place_ends(values, rng, least, top_value):
    shape = values.shape
    index_at = [jax.random.randint(jax.random.fold_in(rng, axis), (), 0, shape[axis]) for axis in range(len(shape))]
    values = values.at[tuple(index_at)].set(least)
    longest = shape.index(max(shape))
    index_at[longest] = (index_at[longest] + 1) % shape[longest]
    return values.at[tuple(index_at)].set(top_value)


def levels(stream_key, extent, cuts, least, high):
    def one(axis_at, parts):
        heights = jax.random.uniform(jax.random.fold_in(jax.random.fold_in(stream_key, 6), axis_at), (parts,), jnp.float32, least / len(cuts), high / len(cuts))
        return jnp.repeat(jnp.exp(heights), extent[axis_at] // parts).reshape((-1,) + (1,) * (len(extent) - axis_at - 1))

    level = one(*cuts[0])
    for cut in cuts[1:]:
        level = level * one(*cut)
    return level


def bell_draw(key, dims, scale, bound, pieces=(), held_as=jnp.bfloat16):
    array = scale * jax.random.normal(key, dims, jnp.float32)
    if pieces:
        array = array * levels(key, dims, pieces, -0.22, 0.18)
    return jnp.clip(array, -bound, bound).astype(held_as)


def setup_inputs(seed: int = 0) -> dict:
    seeds = jax.random.split(jax.random.key(seed), 11)
    features = bell_draw(seeds[0], (NODES, F), 1.0, 6.0, ((0, 256),), jnp.float32)
    send_rows = place_ends(jax.random.randint(seeds[1], (N_DOM, N_ROW, N_DOM, TILE), 0, PANEL), jax.random.fold_in(seeds[1], 1), 0, PANEL - 1).astype(jnp.int32)
    tile_values = bell_draw(seeds[2], (N_DOM, N_ROW, TILES, TILE, TILE), (TILE * TILES_DEV * N_REP // (2 * BLK_DEV)) ** -0.5, 0.125, ((0, 16), (1, 8), (2, 2)), jnp.float32)
    tile_rows = place_ends(jax.random.randint(seeds[3], (N_DOM, N_ROW, TILES), 0, BLK_DEV), jax.random.fold_in(seeds[3], 1), 0, BLK_DEV - 1).astype(jnp.int32)
    tile_cols = place_ends(jax.random.randint(seeds[4], (N_DOM, N_ROW, TILES), 0, COLS), jax.random.fold_in(seeds[4], 1), 0, COLS - 1).astype(jnp.int32)
    tile_counts = draw_tile_counts(jax.random.fold_in(seeds[10], 71), 0)
    history = bell_draw(seeds[6], (N_DOM * N_ROW * N_DOM * TILE, H), 0.5, 4.0, ((0, 128),), jnp.float32)
    weight_one = bell_draw(seeds[7], (F, H), F ** -0.5, 0.5, (), jnp.float32)
    weight_two = bell_draw(seeds[8], (H, H), H ** -0.5, 0.375, (), jnp.float32)
    cotangent = bell_draw(seeds[9], (NODES, H), NODES ** -0.5, 0.0234375, ((0, 128),), jnp.float32)
    return {"features": features, "send_rows": send_rows, "tile_values": tile_values, "tile_rows": tile_rows, "tile_cols": tile_cols, "tile_counts": tile_counts, "history": history, "weight_one": weight_one, "weight_two": weight_two, "cotangent": cotangent}


highest = lax.Precision.HIGHEST

def silu_grad(pre_act):
    sigmoid_value = jax.nn.sigmoid(pre_act)
    return sigmoid_value * (1.0 + pre_act * (1.0 - sigmoid_value))

def live_mask(panel_counts):
    slot_ids = jnp.arange(TILES_DEV * N_REP, dtype=jnp.int32)
    owner_rep = slot_ids // TILES_DEV
    return (slot_ids % TILES_DEV < panel_counts[owner_rep]).astype(jnp.float32)

def panel_sum(values, row_ids, col_ids, live_tiles, extended):
    feature_width = extended.shape[-1]
    blocks = extended.reshape(-1, TILE, feature_width)
    picked = jnp.take(blocks, col_ids, axis=0)
    product = jnp.einsum('tij,tjw->tiw', values, picked, precision=highest) * live_tiles[:, None, None]
    onehot = (row_ids[:, None] == jnp.arange(BLK_DEV, dtype=jnp.int32)[None, :]).astype(jnp.float32)
    summed = jnp.einsum('tb,tiw->biw', onehot, product, precision=highest)
    return summed.reshape(BLK_DEV * TILE, feature_width)

def panel_transpose(values, row_ids, col_ids, live_tiles, upstream_panel):
    feature_width = upstream_panel.shape[-1]
    blocks = upstream_panel.reshape(BLK_DEV, TILE, feature_width)
    picked = jnp.take(blocks, row_ids, axis=0)
    product = jnp.einsum('tji,tjw->tiw', values, picked, precision=highest) * live_tiles[:, None, None]
    onehot = (col_ids[:, None] == jnp.arange(N_ROW * BLK_DEV, dtype=jnp.int32)[None, :]).astype(jnp.float32)
    summed = jnp.einsum('tc,tiw->ciw', onehot, product, precision=highest)
    return summed.reshape(N_ROW * BLK_DEV * TILE, feature_width)

def take_rows(panel, row_list):
    return jnp.take(panel, row_list, axis=0)

def boundary(panels, send_rows):
    picked = jax.vmap(jax.vmap(take_rows))(panels, send_rows)
    return jnp.transpose(picked, (2, 1, 0, 3, 4))

def aggregate(node_rows, halo_rows, tile_values, tile_rows, tile_cols, tile_counts):
    feature_width = node_rows.shape[-1]
    partitions = node_rows.reshape(N_DOM, N_ROW * BLK_DEV * TILE, feature_width)

    def one_panel(flat_index):
        domain = flat_index // N_ROW
        panel_row = flat_index % N_ROW
        extended = jnp.concatenate([partitions[domain], halo_rows[domain, panel_row].reshape(N_DOM * TILE, feature_width)], axis=0)
        return panel_sum(tile_values[domain, panel_row], tile_rows[domain, panel_row], tile_cols[domain, panel_row], live_mask(tile_counts[domain, panel_row]), extended)
    result = lax.map(one_panel, jnp.arange(N_DOM * N_ROW, dtype=jnp.int32))
    return result.reshape(N_DOM * N_ROW * BLK_DEV * TILE, feature_width)

def spread_back(upstream, tile_values, tile_rows, tile_cols, tile_counts):
    feature_width = upstream.shape[-1]
    panels = upstream.reshape(N_DOM, N_ROW, BLK_DEV * TILE, feature_width)

    def one_domain(domain):

        def add_panel(total, panel_row):
            term = panel_transpose(tile_values[domain, panel_row], tile_rows[domain, panel_row], tile_cols[domain, panel_row], live_mask(tile_counts[domain, panel_row]), panels[domain, panel_row])
            return (total + term, None)
        start = jnp.zeros((N_ROW * BLK_DEV * TILE, feature_width), jnp.float32)
        total, unused = lax.scan(add_panel, start, jnp.arange(N_ROW, dtype=jnp.int32))
        return total
    return lax.map(one_domain, jnp.arange(N_DOM, dtype=jnp.int32)).reshape(-1, feature_width)

def reference(features, send_rows, tile_values, tile_rows, tile_cols, tile_counts, history, weight_one, weight_two, cotangent):
    feature_panels = features.reshape(N_DOM, N_ROW, BLK_DEV * TILE, F)
    halo_features = boundary(feature_panels, send_rows)
    agg_one = aggregate(features, halo_features, tile_values, tile_rows, tile_cols, tile_counts)
    pre_act = jnp.dot(agg_one, weight_one, precision=highest, preferred_element_type=jnp.float32)
    hidden = jax.nn.silu(pre_act)
    fresh_halo = boundary(hidden.reshape(N_DOM, N_ROW, BLK_DEV * TILE, H), send_rows).reshape(N_DOM * N_ROW * N_DOM * TILE, H)
    agg_two = aggregate(hidden, history.reshape(N_DOM, N_ROW, N_DOM, TILE, H), tile_values, tile_rows, tile_cols, tile_counts)
    output = jnp.dot(agg_two, weight_two, precision=highest, preferred_element_type=jnp.float32)
    grad_two = jnp.einsum('nf,nh->fh', agg_two, cotangent, precision=highest)
    upstream = jnp.einsum('nh,fh->nf', cotangent, weight_two, precision=highest)
    grad_hidden = spread_back(upstream, tile_values, tile_rows, tile_cols, tile_counts)
    grad_pre = grad_hidden * silu_grad(pre_act)
    grad_one = jnp.einsum('nf,nh->fh', agg_one, grad_pre, precision=highest)
    return (output, grad_one, grad_two, fresh_halo)
```

```python
import jax
import jax.numpy as jnp
from jax import lax
from jax.experimental import pallas as pl
from jax.experimental.pallas import tpu as pltpu
from jax.sharding import PartitionSpec as P

f32 = jnp.float32
bf16 = jnp.bfloat16
TILE = 128
N_DOM, N_ROW, N_REP = 16, 8, 2
OWN = 32
COLS = 48
SLOTS = 64
GROUP = 8
NN = (((1,), (0,)), ((), ()))
TN = (((0,), (0,)), ((), ()))
NT = (((1,), (1,)), ((), ()))
VMEM_LIMIT = 56 * 1024 * 1024
SHIFTS = (0, 1, 7, 4, 2, 6, 3, 5)


def split2(x):
    hi = x.astype(bf16)
    lo = (x - hi.astype(f32)).astype(bf16)
    return hi, lo


def split3(x):
    hi = x.astype(bf16)
    rest = x - hi.astype(f32)
    mid = rest.astype(bf16)
    lo = (rest - mid.astype(f32)).astype(bf16)
    return hi, mid, lo


def mm(a, b, dims):
    return lax.dot_general(a, b, dims, preferred_element_type=f32)


def dot3(a, b, dims):
    a_hi, a_lo = split2(a)
    b_hi, b_lo = split2(b)
    return mm(a_hi, b_hi, dims) + (mm(a_hi, b_lo, dims) + mm(a_lo, b_hi, dims))


def pick_rows(panel, idx_ref, out_ref):
    rhs = jnp.concatenate(split3(panel), axis=1)
    lane = lax.broadcasted_iota(jnp.int32, (TILE, TILE), 1).astype(f32)
    for b in range(idx_ref.shape[0]):
        row = jnp.broadcast_to(idx_ref[b : b + 1, :].astype(f32), (TILE, TILE))
        col = row.T
        marks = [
            jnp.where(col == lane + float(k * TILE), 1.0, 0.0).astype(bf16)
            for k in range(panel.shape[0] // TILE)
        ]
        got = mm(jnp.concatenate(marks, axis=1), rhs, NN)
        out_ref[pl.ds(b * TILE, TILE), :] = (
            got[:, :TILE] + got[:, TILE : 2 * TILE]
        ) + got[:, 2 * TILE :]


def pick_features_kernel(place, mine, other, idx_ref, out_ref):
    q = place[0]
    a, b = mine[...], other[...]
    panel = jnp.concatenate([jnp.where(q == 0, a, b), jnp.where(q == 0, b, a)], axis=0)
    pick_rows(panel, idx_ref, out_ref)


def pick_agg_kernel(place, mine, other, idx_ref, panel_ref, half_ref, out_ref):
    q = place[0]
    panel = mine[...] + other[...]
    panel_ref[...] = panel
    half = panel.shape[0] // 2
    half_ref[...] = jnp.where(q == 0, panel[:half], panel[half:])
    pick_rows(panel, idx_ref, out_ref)


def backward_kernel(rows_s, cols_s, count_s, cot, w2, tiles, out, u_scr):
    g = pl.program_id(0)

    @pl.when(g == 0)
    def _():
        out[...] = jnp.zeros_like(out)
        for b in range(4):
            up = dot3(cot[pl.ds(b * TILE, TILE), :], w2[...], NT)
            hi, lo = split2(up)
            u_scr[b, :TILE, :] = hi
            u_scr[b, TILE:, :] = lo

    count = count_s[0, 0]

    @pl.when(g * GROUP < count)
    def _():
        for i in range(GROUP):
            t = g * GROUP + i
            live = jnp.where(t < count, 1.0, 0.0).astype(f32)
            a_hi, a_lo = split2((tiles[i] * live).T)
            u = u_scr[rows_s[0, t]]
            term = mm(jnp.concatenate([a_hi, a_hi], axis=1), u, NN) + mm(a_lo, u[:TILE], NN)
            c = jnp.minimum(cols_s[0, t], OWN)
            out[c] += term


def forward_tiles(g, rows_s, cols_s, count, tiles, x_scr, acc):
    @pl.when(g * GROUP < count)
    def _():
        for i in range(GROUP):
            t = g * GROUP + i
            live = jnp.where(t < count, 1.0, 0.0).astype(f32)
            a_hi, a_lo = split2(tiles[i] * live)
            x = x_scr[cols_s[0, t]]
            term = mm(jnp.concatenate([a_hi, a_hi], axis=1), x, NN) + mm(a_lo, x[:TILE], NN)
            acc[rows_s[0, t]] += term


def piece_copies(place, mine, theirs, dst, sems):
    q, r = place[0], place[1]
    copies = []
    for n, s in enumerate(SHIFTS):
        base = lax.rem(r + (N_ROW - s), N_ROW) * 4
        for m, (refs, half) in enumerate(((mine, q), (theirs, 1 - q))):
            if refs[n] is None:
                continue
            copies.append(
                pltpu.make_async_copy(
                    refs[n], dst.at[pl.ds(base + half * 2, 2)], sems.at[2 * n + m]
                )
            )
    return copies


def pass_one_kernel(place, rows_s, cols_s, count_s, *refs):
    mine, theirs = refs[:8], refs[8:16]
    halo_mine, halo_theirs, tiles, acc, xf, x_scr, sems = refs[16:]
    g = pl.program_id(0)
    q = place[0]

    @pl.when(g == 0)
    def _():
        copies = piece_copies(place, mine, theirs, xf, sems)
        for m, (ref, half) in enumerate(((halo_mine, q), (halo_theirs, 1 - q))):
            at = pl.multiple_of(half * 64, 64)
            copies.append(
                pltpu.make_async_copy(
                    ref, xf.at[pl.ds(OWN, N_DOM), pl.ds(at, 64), :], sems.at[16 + m]
                )
            )
        for c in copies:
            c.start()
        acc[...] = jnp.zeros_like(acc)
        for c in copies:
            c.wait()

        def body(j, carry):
            for k in range(4):
                hi, lo = split2(xf[j * 4 + k])
                x_scr[j * 4 + k, :TILE, :] = hi
                x_scr[j * 4 + k, TILE:, :] = lo
            return carry

        lax.fori_loop(0, COLS // 4, body, 0)

    forward_tiles(g, rows_s, cols_s, count_s[0, 0], tiles, x_scr, acc)


def layer_two_kernel(place, rows_s, cols_s, count_s, *refs):
    own, mine, theirs = refs[0], refs[1:8], refs[8:15]
    (w1, w2, cot, hist, c_terms, tiles) = refs[15:21]
    (g_keep, g_send, p_keep, p_send) = refs[21:25]
    (xf, h_scr, acc, g_one, sems) = refs[25:]
    g = pl.program_id(0)
    q, r = place[0], place[1]

    @pl.when(g == 0)
    def _():
        copies = piece_copies(place, (None,) + mine, (None,) + theirs, xf, sems)
        copies.append(pltpu.make_async_copy(own, xf.at[pl.ds(r * 4, 4)], sems.at[0]))
        for c in copies:
            c.start()
        acc[...] = jnp.zeros_like(acc)
        g_one[...] = jnp.zeros_like(g_one)
        for c in copies:
            c.wait()

    @pl.when(g < N_ROW)
    def _():
        w_hi, w_lo = split2(w1[...])
        total = jnp.zeros((TILE, w1.shape[1]), f32)
        for b in range(4):
            x = xf[g * 4 + b]
            x_hi, x_lo = split2(x)
            pre = mm(x_hi, w_hi, NN) + (mm(x_hi, w_lo, NN) + mm(x_lo, w_hi, NN))
            sig = 1.0 / (1.0 + jnp.exp(-pre))
            hi, lo = split2(pre * sig)
            h_scr[g * 4 + b, :TILE, :] = hi
            h_scr[g * 4 + b, TILE:, :] = lo
            grad = c_terms[b] * (sig * (1.0 + pre * (1.0 - sig)))
            total += dot3(x, grad, TN)
        g_one[...] += total
        for b in range(2):
            hi, lo = split2(hist[b])
            h_scr[OWN + g * 2 + b, :TILE, :] = hi
            h_scr[OWN + g * 2 + b, TILE:, :] = lo

    @pl.when(g >= N_ROW)
    def _():
        forward_tiles(g - N_ROW, rows_s, cols_s, count_s[0, 0], tiles, h_scr, acc)

    @pl.when(g == 2 * N_ROW - 1)
    def _():
        agg = acc[...].reshape(4 * TILE, -1)
        g_two = dot3(agg, cot[...], TN)
        left = jnp.concatenate([g_one[:, :TILE], g_two[:, :TILE]], axis=0)
        right = jnp.concatenate([g_one[:, TILE:], g_two[:, TILE:]], axis=0)
        g_keep[...] = jnp.where(q == 0, left, right)
        g_send[...] = jnp.where(q == 0, right, left)
        prod = dot3(agg, w2[...], NN)
        low, high = prod[: 2 * TILE], prod[2 * TILE :]
        p_keep[...] = jnp.where(q == 0, low, high)
        p_send[...] = jnp.where(q == 0, high, low)


def fresh_kernel(place, mine, theirs, w1, out):
    q = place[0]
    w_hi, w_lo = split2(w1[...])
    for s in range(mine.shape[0]):
        a, b = mine[s], theirs[s]
        x = jnp.concatenate([jnp.where(q == 0, a, b), jnp.where(q == 0, b, a)], axis=0)
        x_hi, x_lo = split2(x)
        pre = mm(x_hi, w_hi, NN) + (mm(x_hi, w_lo, NN) + mm(x_lo, w_hi, NN))
        out[pl.ds(s * TILE, TILE), :] = pre / (1.0 + jnp.exp(-pre))


SMEM = pl.BlockSpec(memory_space=pltpu.SMEM)
VMEM = pl.BlockSpec(memory_space=pltpu.VMEM)
ANY = pl.BlockSpec(memory_space=pl.ANY)


def params():
    return pltpu.CompilerParams(vmem_limit_bytes=VMEM_LIMIT)


def cost(flops, moved):
    return pl.CostEstimate(flops=flops, bytes_accessed=moved, transcendentals=0)


def swap(x):
    return lax.ppermute(x, "rep", [(0, 1), (1, 0)])


def shift(x, k):
    return lax.ppermute(x, "row", [(i, (i + k) % N_ROW) for i in range(N_ROW)])


def ring_pieces(x):
    a = shift(x, 1)
    b = shift(x, 7)
    f = shift(x, 4)
    a2 = shift(a, 1)
    b2 = shift(b, 7)
    a3 = shift(a, 2)
    b3 = shift(b, 6)
    return [a, b, f, a2, b2, a3, b3]


def blocks(x):
    return x.reshape(-1, TILE, x.shape[-1])


def to_all(x):
    return lax.all_to_all(x, "dom", split_axis=0, concat_axis=0, tiled=True)


def reduce_all(keep, send):
    part = (keep + swap(send)).reshape(N_DOM, -1, TILE)
    part = jnp.sum(to_all(part), axis=0)
    part = jnp.broadcast_to(part[None], (N_ROW,) + part.shape)
    part = lax.all_to_all(part, "row", split_axis=0, concat_axis=0, tiled=True)
    part = jnp.sum(part, axis=0)
    part = jnp.broadcast_to(part[None], (N_DOM,) + part.shape)
    mine = to_all(part).reshape(-1, TILE)
    theirs = swap(mine)
    return mine, theirs


def local(
    features,
    send_rows,
    tile_values,
    tile_rows,
    tile_cols,
    tile_counts,
    history,
    weight_one,
    weight_two,
    cotangent,
):
    f_dim, h_dim = weight_one.shape
    tiles = tile_values.reshape(SLOTS, TILE, TILE)
    rows_s = tile_rows.reshape(1, SLOTS)
    cols_s = tile_cols.reshape(1, SLOTS)
    count_s = tile_counts.reshape(1, 1)
    q = lax.axis_index("rep")
    place = jnp.stack([q, lax.axis_index("row")]).astype(jnp.int32)
    idx = lax.dynamic_slice_in_dim(send_rows.reshape(N_DOM, TILE), q * 64, 64, 1).reshape(8, TILE)

    mine = [features] + ring_pieces(features)
    theirs = [swap(x) for x in mine]
    outgoing = pl.pallas_call(
        pick_features_kernel,
        name="pick_features",
        out_shape=jax.ShapeDtypeStruct((N_DOM * 64, f_dim), f32),
        in_specs=[SMEM, VMEM, VMEM, VMEM],
        out_specs=VMEM,
        compiler_params=params(),
    )(place, features, theirs[0], idx)
    halo_mine = to_all(outgoing.reshape(N_DOM, 64, f_dim))
    halo_theirs = swap(halo_mine)

    tile_spec = pl.BlockSpec((GROUP, TILE, TILE), lambda g: (g, 0, 0))

    c_terms = pl.pallas_call(
        backward_kernel,
        name="backward",
        grid=(SLOTS // GROUP,),
        out_shape=jax.ShapeDtypeStruct((OWN + 1, TILE, h_dim), f32),
        in_specs=[SMEM, SMEM, SMEM, VMEM, VMEM, tile_spec],
        out_specs=pl.BlockSpec((OWN + 1, TILE, h_dim), lambda g: (0, 0, 0)),
        scratch_shapes=[pltpu.VMEM((4, 2 * TILE, h_dim), bf16)],
        compiler_params=params(),
        cost_estimate=cost(6 * SLOTS * TILE * TILE * h_dim, 9 << 20),
    )(rows_s, cols_s, count_s, cotangent, weight_two, tiles)

    part_one = pl.pallas_call(
        pass_one_kernel,
        name="pass_one",
        grid=(SLOTS // GROUP,),
        out_shape=jax.ShapeDtypeStruct((4, TILE, f_dim), f32),
        in_specs=[SMEM] * 4 + [ANY] * 18 + [tile_spec],
        out_specs=pl.BlockSpec((4, TILE, f_dim), lambda g: (0, 0, 0)),
        scratch_shapes=[
            pltpu.VMEM((COLS, TILE, f_dim), f32),
            pltpu.VMEM((COLS, 2 * TILE, f_dim), bf16),
            pltpu.SemaphoreType.DMA((18,)),
        ],
        compiler_params=params(),
    )(
        place,
        rows_s,
        cols_s,
        count_s,
        *[blocks(x) for x in mine],
        *[blocks(x) for x in theirs],
        halo_mine,
        halo_theirs,
        tiles,
    ).reshape(4 * TILE, f_dim)

    panel, half, outgoing_two = pl.pallas_call(
        pick_agg_kernel,
        name="pick_agg",
        out_shape=(
            jax.ShapeDtypeStruct((4 * TILE, f_dim), f32),
            jax.ShapeDtypeStruct((2 * TILE, f_dim), f32),
            jax.ShapeDtypeStruct((N_DOM * 64, f_dim), f32),
        ),
        in_specs=[SMEM, VMEM, VMEM, VMEM],
        out_specs=(VMEM, VMEM, VMEM),
        compiler_params=params(),
    )(place, part_one, swap(part_one), idx)
    agg_mine = ring_pieces(half)
    agg_theirs = [swap(x) for x in agg_mine]
    fresh_mine = to_all(outgoing_two.reshape(N_DOM, 64, f_dim))
    fresh_theirs = swap(fresh_mine)

    last = N_ROW - 1
    g_keep, g_send, p_keep, p_send = pl.pallas_call(
        layer_two_kernel,
        name="layer_two",
        grid=(2 * N_ROW,),
        out_shape=(
            jax.ShapeDtypeStruct((f_dim + h_dim, TILE), f32),
            jax.ShapeDtypeStruct((f_dim + h_dim, TILE), f32),
            jax.ShapeDtypeStruct((2 * TILE, h_dim), f32),
            jax.ShapeDtypeStruct((2 * TILE, h_dim), f32),
        ),
        in_specs=[SMEM] * 4
        + [ANY] * 15
        + [
            VMEM,
            VMEM,
            VMEM,
            pl.BlockSpec((2, TILE, h_dim), lambda g: (jnp.minimum(g, last), 0, 0)),
            pl.BlockSpec((4, TILE, h_dim), lambda g: (jnp.minimum(g, last), 0, 0)),
            pl.BlockSpec((GROUP, TILE, TILE), lambda g: (jnp.maximum(g - N_ROW, 0), 0, 0)),
        ],
        out_specs=(VMEM, VMEM, VMEM, VMEM),
        scratch_shapes=[
            pltpu.VMEM((OWN, TILE, f_dim), f32),
            pltpu.VMEM((COLS, 2 * TILE, h_dim), bf16),
            pltpu.VMEM((4, TILE, h_dim), f32),
            pltpu.VMEM((f_dim, h_dim), f32),
            pltpu.SemaphoreType.DMA((16,)),
        ],
        compiler_params=params(),
    )(
        place,
        rows_s,
        cols_s,
        count_s,
        blocks(panel),
        *[blocks(x) for x in agg_mine],
        *[blocks(x) for x in agg_theirs],
        weight_one,
        weight_two,
        cotangent,
        blocks(history),
        c_terms,
        tiles,
    )

    output = p_keep + swap(p_send)
    mine_g, theirs_g = reduce_all(g_keep, g_send)
    low = jnp.where(q == 0, mine_g, theirs_g)
    high = jnp.where(q == 0, theirs_g, mine_g)
    grads = jnp.concatenate([low, high], axis=1)

    fresh = pl.pallas_call(
        fresh_kernel,
        name="fresh",
        out_shape=jax.ShapeDtypeStruct((N_DOM * TILE, h_dim), f32),
        in_specs=[SMEM, VMEM, VMEM, VMEM],
        out_specs=VMEM,
        compiler_params=params(),
        cost_estimate=cost(6 * N_DOM * TILE * f_dim * h_dim, 4 << 20),
    )(place, fresh_mine, fresh_theirs, weight_one)
    return (output, grads[:f_dim], grads[f_dim:], fresh)


def solution(mesh):
    return jax.shard_map(
        local,
        mesh=mesh,
        in_specs=(
            P(("dom", "row", "rep"), None),
            P("dom", "row", None, None),
            P("dom", "row", "rep", None, None),
            P("dom", "row", "rep"),
            P("dom", "row", "rep"),
            P("dom", "row", "rep"),
            P(("dom", "row"), None),
            P(),
            P(),
            P(("dom", "row"), None),
        ),
        out_specs=(P(("dom", "row", "rep"), None), P(), P(), P(("dom", "row"), None)),
        check_vma=False,
    )
```

```python
import jax
import jax.numpy as jnp
from jax import lax
from jax.experimental import pallas as pl
from jax.experimental.pallas import tpu as pltpu
from jax.sharding import PartitionSpec as P

f32 = jnp.float32
bf16 = jnp.bfloat16
TILE = 128
HALF = 64
N_DOM, N_ROW, N_REP = 16, 8, 2
OWN = 32
COLS = 48
SLOTS = 64
GROUP = 8
NN = (((1,), (0,)), ((), ()))
TN = (((0,), (0,)), ((), ()))
NT = (((1,), (1,)), ((), ()))
VMEM_LIMIT = 56 * 1024 * 1024


def split2(x):
    hi = x.astype(bf16)
    lo = (x - hi.astype(f32)).astype(bf16)
    return hi, lo


def split3(x):
    hi = x.astype(bf16)
    rest = x - hi.astype(f32)
    mid = rest.astype(bf16)
    lo = (rest - mid.astype(f32)).astype(bf16)
    return hi, mid, lo


def mm(a, b, dims):
    return lax.dot_general(a, b, dims, preferred_element_type=f32)


def dot3(a, b, dims):
    a_hi, a_lo = split2(a)
    b_hi, b_lo = split2(b)
    return mm(a_hi, b_hi, dims) + (mm(a_hi, b_lo, dims) + mm(a_lo, b_hi, dims))


def pick_rows(q, panel, idx_ref, out_ref):
    rhs = jnp.concatenate(split3(panel), axis=1)
    lane = lax.broadcasted_iota(jnp.int32, (TILE, TILE), 1).astype(f32)
    for b in range(N_DOM // 2):
        cols = []
        for p in (2 * b, 2 * b + 1):
            col = jnp.broadcast_to(idx_ref[p : p + 1, :].astype(f32), (TILE, TILE)).T
            cols.append(jnp.where(q == 0, col[:HALF], col[HALF:]))
        col = jnp.concatenate(cols, axis=0)
        marks = [
            jnp.where(col == lane + float(k * TILE), 1.0, 0.0).astype(bf16)
            for k in range(panel.shape[0] // TILE)
        ]
        got = mm(jnp.concatenate(marks, axis=1), rhs, NN)
        out_ref[pl.ds(b * TILE, TILE), :] = (
            got[:, :TILE] + got[:, TILE : 2 * TILE]
        ) + got[:, 2 * TILE :]


def pick_features_kernel(place, mine, other, idx_ref, out_ref):
    q = place[0]
    a, b = mine[...], other[...]
    panel = jnp.concatenate([jnp.where(q == 0, a, b), jnp.where(q == 0, b, a)], axis=0)
    pick_rows(q, panel, idx_ref, out_ref)


def pick_agg_kernel(place, mine, other, idx_ref, panel_ref, out_ref):
    q = place[0]
    panel = mine[...] + other[...]
    size = panel.shape[0] // 2
    panel_ref[:size, :] = jnp.where(q == 0, panel[:size], panel[size:])
    panel_ref[size:, :] = jnp.where(q == 0, panel[size:], panel[:size])
    pick_rows(q, panel, idx_ref, out_ref)


def tile_copies(tiles_hbm, tiles, sems):
    return [
        pltpu.make_async_copy(
            tiles_hbm.at[pl.ds(k * GROUP, GROUP)], tiles.at[pl.ds(k * GROUP, GROUP)], sems.at[k]
        )
        for k in range(SLOTS // GROUP)
    ]


def each_tile(count_s, tiles_hbm, tiles, sems, one_tile):
    count = count_s[0, 0]

    def body(g, carry):
        part = pl.ds(g * GROUP, GROUP)
        pltpu.make_async_copy(tiles_hbm.at[part], tiles.at[part], sems.at[g]).wait()

        @pl.when(g * GROUP < count)
        def _():
            for i in range(GROUP):
                t = g * GROUP + i
                live = jnp.where(t < count, 1.0, 0.0).astype(f32)
                one_tile(t, tiles[t] * live)

        return carry

    lax.fori_loop(0, SLOTS // GROUP, body, 0)


def backward_kernel(rows_s, cols_s, count_s, cot, w2, tiles_hbm, out, u_scr, tiles, sems):
    for c in tile_copies(tiles_hbm, tiles, sems):
        c.start()
    out[...] = jnp.zeros_like(out)
    for b in range(4):
        hi, lo = split2(dot3(cot[pl.ds(b * TILE, TILE), :], w2[...], NT))
        u_scr[b, :TILE, :] = hi
        u_scr[b, TILE:, :] = lo

    def one_tile(t, a):
        a_hi, a_lo = split2(a)
        u = u_scr[rows_s[0, t]]
        term = mm(jnp.concatenate([a_hi, a_hi], axis=0), u, TN) + mm(a_lo, u[:TILE], TN)
        out[jnp.minimum(cols_s[0, t], OWN)] += term

    each_tile(count_s, tiles_hbm, tiles, sems, one_tile)


def forward_tiles(rows_s, cols_s, count_s, tiles_hbm, tiles, sems, x_scr, acc):
    def one_tile(t, a):
        a_hi, a_lo = split2(a)
        x = x_scr[cols_s[0, t]]
        term = mm(jnp.concatenate([a_hi, a_hi], axis=1), x, NN) + mm(a_lo, x[:TILE], NN)
        acc[rows_s[0, t]] += term

    each_tile(count_s, tiles_hbm, tiles, sems, one_tile)


def piece_copies(place, own, mine, theirs, dst, sems):
    q, r = place[0], place[1]
    side = 1 - 2 * q
    parts = [(own[0], r, q), (own[1], r, 1 - q)]
    for refs, way, half in ((mine, side, q), (theirs, -side, 1 - q)):
        for s in (1, 2, 3):
            row = lax.rem(r + N_ROW - way * s, N_ROW)
            parts.append((refs[s - 1].at[pl.ds(0, 2)], row, half))
            parts.append((refs[s - 1].at[pl.ds(2, 2)], row, 1 - half))
        parts.append((refs[3], lax.rem(r + 4, N_ROW), half))
    return [
        pltpu.make_async_copy(ref, dst.at[pl.ds(row * 4 + half * 2, 2)], sems.at[k])
        for k, (ref, row, half) in enumerate(parts)
    ]


def pass_one_kernel(place, rows_s, cols_s, count_s, *refs):
    own, other, mine, theirs = refs[0], refs[1], refs[2:6], refs[6:10]
    halo_mine, halo_theirs, tiles_hbm, acc, xf, x_scr, tiles, sems, tile_sems = refs[10:]
    q = place[0]
    copies = piece_copies(place, (own, other), mine, theirs, xf, sems)
    for m, (ref, half) in enumerate(((halo_mine, q), (halo_theirs, 1 - q))):
        at = pl.multiple_of(half * HALF, HALF)
        copies.append(
            pltpu.make_async_copy(
                ref, xf.at[pl.ds(OWN, N_DOM), pl.ds(at, HALF), :], sems.at[16 + m]
            )
        )
    for c in copies + tile_copies(tiles_hbm, tiles, tile_sems):
        c.start()
    acc[...] = jnp.zeros_like(acc)
    for c in copies:
        c.wait()

    def body(j, carry):
        for k in range(4):
            hi, lo = split2(xf[j * 4 + k])
            x_scr[j * 4 + k, :TILE, :] = hi
            x_scr[j * 4 + k, TILE:, :] = lo
        return carry

    lax.fori_loop(0, COLS // 4, body, 0)
    forward_tiles(rows_s, cols_s, count_s, tiles_hbm, tiles, tile_sems, x_scr, acc)


def layer_two_kernel(place, rows_s, cols_s, count_s, *refs):
    own, mine, theirs = refs[0], refs[1:5], refs[5:9]
    (w1, w2, cot, hist_hbm, c_hbm, tiles_hbm) = refs[9:15]
    (g_keep, g_send, p_keep, p_send) = refs[15:19]
    (xf, h_scr, acc, g_one, hist, c_terms, tiles, sems, tile_sems, c_sems) = refs[19:]
    q = place[0]

    def c_copy(g):
        part = pl.ds(g * 4, 4)
        return pltpu.make_async_copy(c_hbm.at[part], c_terms.at[part], c_sems.at[g])

    copies = piece_copies(place, (own.at[pl.ds(0, 2)], own.at[pl.ds(2, 2)]), mine, theirs, xf, sems)
    hist_copy = pltpu.make_async_copy(hist_hbm, hist, sems.at[16])
    for c in copies:
        c.start()
    for g in range(N_ROW):
        c_copy(g).start()
    hist_copy.start()
    for c in tile_copies(tiles_hbm, tiles, tile_sems):
        c.start()
    acc[...] = jnp.zeros_like(acc)
    g_one[...] = jnp.zeros_like(g_one)
    for c in copies:
        c.wait()

    def panel_step(g, carry):
        c_copy(g).wait()
        w_hi, w_lo = split2(w1[...])
        total = jnp.zeros((TILE, w1.shape[1]), f32)
        for b in range(4):
            x = xf[g * 4 + b]
            x_hi, x_lo = split2(x)
            pre = mm(x_hi, w_hi, NN) + (mm(x_hi, w_lo, NN) + mm(x_lo, w_hi, NN))
            sig = 1.0 / (1.0 + jnp.exp(-pre))
            hi, lo = split2(pre * sig)
            h_scr[g * 4 + b, :TILE, :] = hi
            h_scr[g * 4 + b, TILE:, :] = lo
            grad = c_terms[g * 4 + b] * (sig * (1.0 + pre * (1.0 - sig)))
            total += dot3(x, grad, TN)
        g_one[...] += total
        return carry

    lax.fori_loop(0, N_ROW, panel_step, 0)
    hist_copy.wait()

    def hist_step(g, carry):
        for b in range(2):
            hi, lo = split2(hist[g * 2 + b])
            h_scr[OWN + g * 2 + b, :TILE, :] = hi
            h_scr[OWN + g * 2 + b, TILE:, :] = lo
        return carry

    lax.fori_loop(0, N_DOM // 2, hist_step, 0)
    forward_tiles(rows_s, cols_s, count_s, tiles_hbm, tiles, tile_sems, h_scr, acc)

    agg = acc[...].reshape(4 * TILE, -1)
    g_two = dot3(agg, cot[...], TN)
    left = jnp.concatenate([g_one[:, :TILE], g_two[:, :TILE]], axis=0)
    right = jnp.concatenate([g_one[:, TILE:], g_two[:, TILE:]], axis=0)
    g_keep[...] = jnp.where(q == 0, left, right)
    g_send[...] = jnp.where(q == 0, right, left)
    prod = dot3(agg, w2[...], NN)
    low, high = prod[: 2 * TILE], prod[2 * TILE :]
    p_keep[...] = jnp.where(q == 0, low, high)
    p_send[...] = jnp.where(q == 0, high, low)


def fresh_kernel(place, mine, theirs, w1, out):
    q = place[0]
    w_hi, w_lo = split2(w1[...])
    for s in range(mine.shape[0]):
        a, b = mine[s], theirs[s]
        x = jnp.concatenate([jnp.where(q == 0, a, b), jnp.where(q == 0, b, a)], axis=0)
        x_hi, x_lo = split2(x)
        pre = mm(x_hi, w_hi, NN) + (mm(x_hi, w_lo, NN) + mm(x_lo, w_hi, NN))
        out[pl.ds(s * TILE, TILE), :] = pre / (1.0 + jnp.exp(-pre))


SMEM = pl.BlockSpec(memory_space=pltpu.SMEM)
VMEM = pl.BlockSpec(memory_space=pltpu.VMEM)
ANY = pl.BlockSpec(memory_space=pl.ANY)


def params():
    return pltpu.CompilerParams(vmem_limit_bytes=VMEM_LIMIT)


def cost(flops, moved):
    return pl.CostEstimate(flops=flops, bytes_accessed=moved, transcendentals=0)


def swap(x):
    return lax.ppermute(x, "rep", [(0, 1), (1, 0)])


def along(x, k):
    pairs = []
    for row in range(N_ROW):
        for core in range(N_REP):
            to = row - k if core else row + k
            pairs.append((row * N_REP + core, to % N_ROW * N_REP + core))
    return lax.ppermute(x, ("row", "rep"), pairs)


def together(*xs):
    return lax.optimization_barrier(xs)


def blocks(x):
    return x.reshape(-1, TILE, x.shape[-1])


def to_all(x):
    return lax.all_to_all(x, "dom", split_axis=0, concat_axis=0, tiled=True)


def local(
    features,
    send_rows,
    tile_values,
    tile_rows,
    tile_cols,
    tile_counts,
    history,
    weight_one,
    weight_two,
    cotangent,
):
    f_dim, h_dim = weight_one.shape
    half_rows = features.shape[0]
    tiles = tile_values.reshape(SLOTS, TILE, TILE)
    rows_s = tile_rows.reshape(1, SLOTS)
    cols_s = tile_cols.reshape(1, SLOTS)
    count_s = tile_counts.reshape(1, 1)
    idx = send_rows.reshape(N_DOM, TILE)
    q = lax.axis_index("rep")
    place = jnp.stack([q, lax.axis_index("row")]).astype(jnp.int32)
    tile_scr = [pltpu.VMEM((SLOTS, TILE, TILE), f32)]
    tile_sems = [pltpu.SemaphoreType.DMA((SLOTS // GROUP,))]

    def backward(count_s):
        return pl.pallas_call(
            backward_kernel,
            name="backward",
            out_shape=jax.ShapeDtypeStruct((OWN + 1, TILE, h_dim), f32),
            in_specs=[SMEM, SMEM, SMEM, VMEM, VMEM, ANY],
            out_specs=VMEM,
            scratch_shapes=[pltpu.VMEM((4, 2 * TILE, h_dim), bf16)] + tile_scr + tile_sems,
            compiler_params=params(),
            cost_estimate=cost(6 * SLOTS * TILE * TILE * h_dim, 9 << 20),
        )(rows_s, cols_s, count_s, cotangent, weight_two, tiles)

    other = swap(features)
    first, second = along(features, 1), along(other, 1)
    outgoing = pl.pallas_call(
        pick_features_kernel,
        name="pick_features",
        out_shape=jax.ShapeDtypeStruct((N_DOM * HALF, f_dim), f32),
        in_specs=[SMEM, VMEM, VMEM, VMEM],
        out_specs=VMEM,
        compiler_params=params(),
        cost_estimate=cost(1 << 20, 1 << 20),
    )(place, features, other, idx)
    first, second, outgoing = together(first, second, outgoing)
    one = jnp.concatenate([first, second])
    halo_mine = to_all(outgoing.reshape(N_DOM, HALF, f_dim))
    two, three, four, theirs_one = together(
        along(one, 1),
        along(one, 2),
        along(first, 3),
        swap(one),
    )
    mine = [one, two, three, four]
    theirs = [theirs_one, swap(two), swap(three), swap(four)]
    halo_mine, *theirs = together(halo_mine, *theirs)
    halo_theirs = swap(halo_mine)

    part_one = pl.pallas_call(
        pass_one_kernel,
        name="pass_one",
        out_shape=jax.ShapeDtypeStruct((4, TILE, f_dim), f32),
        in_specs=[SMEM] * 4 + [ANY] * 13,
        out_specs=VMEM,
        scratch_shapes=[
            pltpu.VMEM((COLS, TILE, f_dim), f32),
            pltpu.VMEM((COLS, 2 * TILE, f_dim), bf16),
        ]
        + tile_scr
        + [pltpu.SemaphoreType.DMA((18,))]
        + tile_sems,
        compiler_params=params(),
    )(
        place,
        rows_s,
        cols_s,
        count_s,
        *[blocks(x) for x in [features, other] + mine + theirs],
        halo_mine,
        halo_theirs,
        tiles,
    ).reshape(4 * TILE, f_dim)

    panel, outgoing_two = pl.pallas_call(
        pick_agg_kernel,
        name="pick_agg",
        out_shape=(
            jax.ShapeDtypeStruct((4 * TILE, f_dim), f32),
            jax.ShapeDtypeStruct((N_DOM * HALF, f_dim), f32),
        ),
        in_specs=[SMEM, VMEM, VMEM, VMEM],
        out_specs=(VMEM, VMEM),
        compiler_params=params(),
    )(place, part_one, swap(part_one), idx)
    fresh_mine = to_all(outgoing_two.reshape(N_DOM, HALF, f_dim))
    one, count_b = together(along(panel, 1), count_s)
    c_terms = backward(count_b)
    two, three, four, theirs_one, c_terms = together(
        along(one, 1),
        along(one, 2),
        along(one[:half_rows], 3),
        swap(one),
        c_terms,
    )
    agg_mine = [one, two, three, four]
    agg_theirs = [theirs_one, swap(two), swap(three), swap(four)]
    fresh_mine, *agg_theirs = together(fresh_mine, *agg_theirs)
    g_keep, g_send, p_keep, p_send = pl.pallas_call(
        layer_two_kernel,
        name="layer_two",
        out_shape=(
            jax.ShapeDtypeStruct((f_dim + h_dim, TILE), f32),
            jax.ShapeDtypeStruct((f_dim + h_dim, TILE), f32),
            jax.ShapeDtypeStruct((2 * TILE, h_dim), f32),
            jax.ShapeDtypeStruct((2 * TILE, h_dim), f32),
        ),
        in_specs=[SMEM] * 4 + [ANY] * 9 + [VMEM] * 3 + [ANY] * 3,
        out_specs=(VMEM, VMEM, VMEM, VMEM),
        scratch_shapes=[
            pltpu.VMEM((OWN, TILE, f_dim), f32),
            pltpu.VMEM((COLS, 2 * TILE, h_dim), bf16),
            pltpu.VMEM((4, TILE, h_dim), f32),
            pltpu.VMEM((f_dim, h_dim), f32),
            pltpu.VMEM((N_DOM, TILE, h_dim), f32),
            pltpu.VMEM((OWN, TILE, h_dim), f32),
        ]
        + tile_scr
        + [pltpu.SemaphoreType.DMA((18,))]
        + tile_sems
        + [pltpu.SemaphoreType.DMA((N_ROW,))],
        compiler_params=params(),
        cost_estimate=cost(8 << 30, 16 << 20),
    )(
        place,
        rows_s,
        cols_s,
        count_s,
        *[blocks(x) for x in [panel] + agg_mine + agg_theirs],
        weight_one,
        weight_two,
        cotangent,
        blocks(history),
        c_terms,
        tiles,
    )

    fresh_mine, g_keep = together(fresh_mine, g_keep)
    fresh_theirs = swap(fresh_mine)
    output = p_keep + swap(p_send)
    fresh = pl.pallas_call(
        fresh_kernel,
        name="fresh",
        out_shape=jax.ShapeDtypeStruct((N_DOM * TILE, h_dim), f32),
        in_specs=[SMEM, VMEM, VMEM, VMEM],
        out_specs=VMEM,
        compiler_params=params(),
        cost_estimate=cost(6 * N_DOM * TILE * f_dim * h_dim, 4 << 20),
    )(place, fresh_mine, fresh_theirs, weight_one)
    part = to_all((g_keep + swap(g_send)).reshape(N_DOM, -1, TILE))
    part = jnp.sum(part, axis=0)
    part = jnp.broadcast_to(part[None], (N_ROW,) + part.shape)
    part = lax.all_to_all(part, "row", split_axis=0, concat_axis=0, tiled=True)
    part, fresh = together(part, fresh)
    part = jnp.sum(part, axis=0)
    part = jnp.broadcast_to(part[None], (N_DOM,) + part.shape)
    mine_g, output = together(to_all(part).reshape(-1, TILE), output)
    theirs_g = swap(mine_g)
    low = jnp.where(q == 0, mine_g, theirs_g)
    high = jnp.where(q == 0, theirs_g, mine_g)
    grads = jnp.concatenate([low, high], axis=1)
    return (output, grads[:f_dim], grads[f_dim:], fresh)


def solution(mesh):
    return jax.shard_map(
        local,
        mesh=mesh,
        in_specs=(
            P(("dom", "row", "rep"), None),
            P("dom", "row", None, None),
            P("dom", "row", "rep", None, None),
            P("dom", "row", "rep"),
            P("dom", "row", "rep"),
            P("dom", "row", "rep"),
            P(("dom", "row"), None),
            P(),
            P(),
            P(("dom", "row"), None),
        ),
        out_specs=(P(("dom", "row", "rep"), None), P(), P(), P(("dom", "row"), None)),
        check_vma=False,
    )
```

```python
import jax
import jax.numpy as jnp
from jax import lax
from jax.experimental import pallas as pl
from jax.experimental.pallas import tpu as pltpu
from jax.sharding import PartitionSpec as P

f32 = jnp.float32
bf16 = jnp.bfloat16
TILE = 128
HALF = 64
N_DOM, N_ROW, N_REP = 16, 8, 2
OWN = 32
COLS = 48
SLOTS = 64
GROUP = 8
NN = (((1,), (0,)), ((), ()))
TN = (((0,), (0,)), ((), ()))
NT = (((1,), (1,)), ((), ()))
VMEM_LIMIT = 56 * 1024 * 1024


def split2(x):
    hi = x.astype(bf16)
    lo = (x - hi.astype(f32)).astype(bf16)
    return hi, lo


def split3(x):
    hi = x.astype(bf16)
    rest = x - hi.astype(f32)
    mid = rest.astype(bf16)
    lo = (rest - mid.astype(f32)).astype(bf16)
    return hi, mid, lo


def mm(a, b, dims):
    return lax.dot_general(a, b, dims, preferred_element_type=f32)


def dot3(a, b, dims):
    a_hi, a_lo = split2(a)
    b_hi, b_lo = split2(b)
    return mm(a_hi, b_hi, dims) + (mm(a_hi, b_lo, dims) + mm(a_lo, b_hi, dims))


def pick_rows(q, panel, idx_ref, out_ref):
    rhs = jnp.concatenate(split3(panel), axis=1)
    lane = lax.broadcasted_iota(jnp.int32, (TILE, TILE), 1).astype(f32)
    for b in range(N_DOM // 2):
        cols = []
        for p in (2 * b, 2 * b + 1):
            col = jnp.broadcast_to(idx_ref[p : p + 1, :].astype(f32), (TILE, TILE)).T
            cols.append(jnp.where(q == 0, col[:HALF], col[HALF:]))
        col = jnp.concatenate(cols, axis=0)
        marks = [
            jnp.where(col == lane + float(k * TILE), 1.0, 0.0).astype(bf16)
            for k in range(panel.shape[0] // TILE)
        ]
        got = mm(jnp.concatenate(marks, axis=1), rhs, NN)
        out_ref[pl.ds(b * TILE, TILE), :] = (
            got[:, :TILE] + got[:, TILE : 2 * TILE]
        ) + got[:, 2 * TILE :]


def pick_kernel(place, mine, other, idx_ref, out_ref):
    q = place[0]
    a, b = mine[...], other[...]
    panel = jnp.concatenate([jnp.where(q == 0, a, b), jnp.where(q == 0, b, a)], axis=0)
    pick_rows(q, panel, idx_ref, out_ref)


def tile_copies(tiles_hbm, tiles, sems):
    return [
        pltpu.make_async_copy(
            tiles_hbm.at[pl.ds(k * GROUP, GROUP)], tiles.at[pl.ds(k * GROUP, GROUP)], sems.at[k]
        )
        for k in range(SLOTS // GROUP)
    ]


def each_tile(count_s, tiles_hbm, tiles, sems, one_tile):
    count = count_s[0, 0]

    def body(g, carry):
        part = pl.ds(g * GROUP, GROUP)
        pltpu.make_async_copy(tiles_hbm.at[part], tiles.at[part], sems.at[g]).wait()

        @pl.when(g * GROUP < count)
        def _():
            for i in range(GROUP):
                t = g * GROUP + i
                live = jnp.where(t < count, 1.0, 0.0).astype(f32)
                one_tile(t, tiles[t] * live)

        return carry

    lax.fori_loop(0, SLOTS // GROUP, body, 0)


def backward_kernel(rows_s, cols_s, count_s, cot, w2, tiles_hbm, out, u_scr, tiles, sems):
    for c in tile_copies(tiles_hbm, tiles, sems):
        c.start()
    out[...] = jnp.zeros_like(out)
    for b in range(4):
        hi, lo = split2(dot3(cot[pl.ds(b * TILE, TILE), :], w2[...], NT))
        u_scr[b, :TILE, :] = hi
        u_scr[b, TILE:, :] = lo

    def one_tile(t, a):
        a_hi, a_lo = split2(a)
        u = u_scr[rows_s[0, t]]
        term = mm(jnp.concatenate([a_hi, a_hi], axis=0), u, TN) + mm(a_lo, u[:TILE], TN)
        out[jnp.minimum(cols_s[0, t], OWN)] += term

    each_tile(count_s, tiles_hbm, tiles, sems, one_tile)


def forward_tiles(rows_s, cols_s, count_s, tiles_hbm, tiles, sems, x_scr, acc):
    def one_tile(t, a):
        a_hi, a_lo = split2(a)
        x = x_scr[cols_s[0, t]]
        term = mm(jnp.concatenate([a_hi, a_hi], axis=1), x, NN) + mm(a_lo, x[:TILE], NN)
        acc[rows_s[0, t]] += term

    each_tile(count_s, tiles_hbm, tiles, sems, one_tile)


def piece_copies(place, own, mine, theirs, dst, sems):
    q, r = place[0], place[1]
    side = 1 - 2 * q
    parts = [(own[0], r, q), (own[1], r, 1 - q)]
    for refs, way, half in ((mine, side, q), (theirs, -side, 1 - q)):
        for s in (1, 2, 3):
            row = lax.rem(r + N_ROW - way * s, N_ROW)
            parts.append((refs[s - 1].at[pl.ds(0, 2)], row, half))
            parts.append((refs[s - 1].at[pl.ds(2, 2)], row, 1 - half))
        parts.append((refs[3], lax.rem(r + 4, N_ROW), half))
    return [
        pltpu.make_async_copy(ref, dst.at[pl.ds(row * 4 + half * 2, 2)], sems.at[k])
        for k, (ref, row, half) in enumerate(parts)
    ]


def pass_one_kernel(place, rows_s, cols_s, count_s, *refs):
    own, other, mine, theirs = refs[0], refs[1], refs[2:6], refs[6:10]
    halo_mine, halo_theirs, tiles_hbm, acc, xf, x_scr, tiles, sems, tile_sems = refs[10:]
    q = place[0]
    copies = piece_copies(place, (own, other), mine, theirs, xf, sems)
    for m, (ref, half) in enumerate(((halo_mine, q), (halo_theirs, 1 - q))):
        at = pl.multiple_of(half * HALF, HALF)
        copies.append(
            pltpu.make_async_copy(
                ref, xf.at[pl.ds(OWN, N_DOM), pl.ds(at, HALF), :], sems.at[16 + m]
            )
        )
    for c in copies + tile_copies(tiles_hbm, tiles, tile_sems):
        c.start()
    acc[...] = jnp.zeros_like(acc)
    for c in copies:
        c.wait()

    def body(j, carry):
        for k in range(4):
            hi, lo = split2(xf[j * 4 + k])
            x_scr[j * 4 + k, :TILE, :] = hi
            x_scr[j * 4 + k, TILE:, :] = lo
        return carry

    lax.fori_loop(0, COLS // 4, body, 0)
    forward_tiles(rows_s, cols_s, count_s, tiles_hbm, tiles, tile_sems, x_scr, acc)


def hidden_step(x, terms, w_hi, w_lo, h_ref, at, n):
    total = jnp.zeros((TILE, w_hi.shape[1]), f32)
    for b in range(n):
        x_b = x[b]
        x_hi, x_lo = split2(x_b)
        pre = mm(x_hi, w_hi, NN) + (mm(x_hi, w_lo, NN) + mm(x_lo, w_hi, NN))
        sig = 1.0 / (1.0 + jnp.exp(-pre))
        hi, lo = split2(pre * sig)
        h_ref[at + b, :TILE, :] = hi
        h_ref[at + b, TILE:, :] = lo
        grad = terms[b] * (sig * (1.0 + pre * (1.0 - sig)))
        total += dot3(x_b, grad, TN)
    return total


def early_kernel(place, own, one, their_one, w1, c_hbm, hidden, g_out, c_terms, sems):
    q, r = place[0], place[1]
    side = 1 - 2 * q
    copies = []
    for k, (row, half) in enumerate(early_parts(r, q, side)):
        for h in (0, 1):
            at = row * 4 + 2 * (half if h == 0 else 1 - half)
            copies.append(
                pltpu.make_async_copy(
                    c_hbm.at[pl.ds(at, 2)], c_terms.at[pl.ds(4 * k + 2 * h, 2)], sems.at[2 * k + h]
                )
            )
    for c in copies:
        c.start()
    w_hi, w_lo = split2(w1[...])
    total = jnp.zeros(g_out.shape, f32)
    for k, x in enumerate((own, one, their_one)):
        copies[2 * k].wait()
        copies[2 * k + 1].wait()
        total += hidden_step(x, c_terms.at[pl.ds(4 * k, 4)], w_hi, w_lo, hidden, 4 * k, 4)
    g_out[...] = total


def early_parts(r, q, side):
    below = lax.rem(r + N_ROW - side, N_ROW)
    above = lax.rem(r + N_ROW + side, N_ROW)
    return ((r, q), (below, q), (above, 1 - q))


def layer_two_kernel(place, rows_s, cols_s, count_s, *refs):
    mine, theirs = refs[0:3], refs[3:6]
    (early, g_early, w1, w2, cot, hist_hbm, c_hbm, tiles_hbm) = refs[6:14]
    grads, p_keep, p_send = refs[14:17]
    (xf, h_scr, acc, g_one, hist, c_terms, tiles, sems, tile_sems, c_sems) = refs[17:]
    q, r = place[0], place[1]
    side = 1 - 2 * q
    parts = []
    for refs_m, way, half in ((mine, side, q), (theirs, -side, 1 - q)):
        for n, s in ((0, 2), (1, 3)):
            slot = lax.rem(2 * N_ROW - way * s, N_ROW) - 2
            parts.append((refs_m[n].at[pl.ds(0, 2)], slot, half))
            parts.append((refs_m[n].at[pl.ds(2, 2)], slot, 1 - half))
        parts.append((refs_m[2], 2, half))
    copies = [
        pltpu.make_async_copy(ref, xf.at[pl.ds(slot * 4 + half * 2, 2)], sems.at[k])
        for k, (ref, slot, half) in enumerate(parts)
    ]
    late = []
    for k, (row, half) in enumerate(early_parts(r, q, side)):
        for h in (0, 1):
            at = row * 4 + 2 * (half if h == 0 else 1 - half)
            late.append(
                pltpu.make_async_copy(
                    early.at[pl.ds(4 * k + 2 * h, 2)], h_scr.at[pl.ds(at, 2)], sems.at[10 + 2 * k + h]
                )
            )
    late.append(pltpu.make_async_copy(hist_hbm, hist, sems.at[16]))

    def row_of(g):
        return lax.rem(r + 2 + g, N_ROW)

    def c_copy(g):
        return pltpu.make_async_copy(
            c_hbm.at[pl.ds(row_of(g) * 4, 4)], c_terms.at[pl.ds(g * 4, 4)], c_sems.at[g]
        )

    for c in copies:
        c.start()
    for g in range(5):
        c_copy(g).start()
    for c in late + tile_copies(tiles_hbm, tiles, tile_sems):
        c.start()
    acc[...] = jnp.zeros_like(acc)
    g_one[...] = g_early[...]
    w_hi, w_lo = split2(w1[...])
    for c in copies:
        c.wait()

    def panel_step(g, carry):
        c_copy(g).wait()
        part = pl.ds(g * 4, 4)
        g_one[...] += hidden_step(xf.at[part], c_terms.at[part], w_hi, w_lo, h_scr, row_of(g) * 4, 4)
        return carry

    lax.fori_loop(0, 5, panel_step, 0)
    for c in late:
        c.wait()

    def hist_step(g, carry):
        for b in range(2):
            hi, lo = split2(hist[g * 2 + b])
            h_scr[OWN + g * 2 + b, :TILE, :] = hi
            h_scr[OWN + g * 2 + b, TILE:, :] = lo
        return carry

    lax.fori_loop(0, N_DOM // 2, hist_step, 0)
    forward_tiles(rows_s, cols_s, count_s, tiles_hbm, tiles, tile_sems, h_scr, acc)

    agg = acc[...].reshape(4 * TILE, -1)
    g_two = dot3(agg, cot[...], TN)
    for h in (0, 1):
        cols = pl.ds(h * TILE, TILE)
        grads[: g_one.shape[0] // 8, h] = g_one[:, cols].reshape(-1, 8, TILE)
        grads[g_one.shape[0] // 8 :, h] = g_two[:, h * TILE : (h + 1) * TILE].reshape(-1, 8, TILE)
    prod = dot3(agg, w2[...], NN)
    low, high = prod[: 2 * TILE], prod[2 * TILE :]
    p_keep[...] = jnp.where(q == 0, low, high)
    p_send[...] = jnp.where(q == 0, high, low)


def fresh_kernel(place, mine, theirs, w1, out):
    q = place[0]
    w_hi, w_lo = split2(w1[...])
    for s in range(mine.shape[0]):
        a, b = mine[s], theirs[s]
        x = jnp.concatenate([jnp.where(q == 0, a, b), jnp.where(q == 0, b, a)], axis=0)
        x_hi, x_lo = split2(x)
        pre = mm(x_hi, w_hi, NN) + (mm(x_hi, w_lo, NN) + mm(x_lo, w_hi, NN))
        out[pl.ds(s * TILE, TILE), :] = pre / (1.0 + jnp.exp(-pre))


SMEM = pl.BlockSpec(memory_space=pltpu.SMEM)
VMEM = pl.BlockSpec(memory_space=pltpu.VMEM)
ANY = pl.BlockSpec(memory_space=pl.ANY)


def params():
    return pltpu.CompilerParams(vmem_limit_bytes=VMEM_LIMIT)


def cost(flops, moved):
    return pl.CostEstimate(flops=flops, bytes_accessed=moved, transcendentals=0)


def swap(x):
    return lax.ppermute(x, "rep", [(0, 1), (1, 0)])


def along(x, k):
    pairs = []
    for row in range(N_ROW):
        for core in range(N_REP):
            to = row - k if core else row + k
            pairs.append((row * N_REP + core, to % N_ROW * N_REP + core))
    return lax.ppermute(x, ("row", "rep"), pairs)


def together(*xs):
    return lax.optimization_barrier(xs)


def blocks(x):
    return x.reshape(-1, TILE, x.shape[-1])


def to_all(x):
    return lax.all_to_all(x, "dom", split_axis=0, concat_axis=0, tiled=True)


def local(
    features,
    send_rows,
    tile_values,
    tile_rows,
    tile_cols,
    tile_counts,
    history,
    weight_one,
    weight_two,
    cotangent,
):
    f_dim, h_dim = weight_one.shape
    half_rows = features.shape[0]
    tiles = tile_values.reshape(SLOTS, TILE, TILE)
    rows_s = tile_rows.reshape(1, SLOTS)
    cols_s = tile_cols.reshape(1, SLOTS)
    count_s = tile_counts.reshape(1, 1)
    idx = send_rows.reshape(N_DOM, TILE)
    q = lax.axis_index("rep")
    place = jnp.stack([q, lax.axis_index("row")]).astype(jnp.int32)
    tile_scr = [pltpu.VMEM((SLOTS, TILE, TILE), f32)]
    tile_sems = [pltpu.SemaphoreType.DMA((SLOTS // GROUP,))]

    def backward(count_s):
        return pl.pallas_call(
            backward_kernel,
            name="backward",
            out_shape=jax.ShapeDtypeStruct((OWN + 1, TILE, h_dim), f32),
            in_specs=[SMEM, SMEM, SMEM, VMEM, VMEM, ANY],
            out_specs=VMEM,
            scratch_shapes=[pltpu.VMEM((4, 2 * TILE, h_dim), bf16)] + tile_scr + tile_sems,
            compiler_params=params(),
            cost_estimate=cost(6 * SLOTS * TILE * TILE * h_dim, 9 << 20),
        )(rows_s, cols_s, count_s, cotangent, weight_two, tiles)

    def pick_call(name, mine, mine_at, other, other_at):
        return pl.pallas_call(
            pick_kernel,
            name=name,
            grid=(1,),
            out_shape=jax.ShapeDtypeStruct((N_DOM * HALF, f_dim), f32),
            in_specs=[
                SMEM,
                pl.BlockSpec((half_rows, f_dim), lambda g: mine_at),
                pl.BlockSpec((half_rows, f_dim), lambda g: other_at),
                VMEM,
            ],
            out_specs=VMEM,
            compiler_params=params(),
            cost_estimate=cost(1 << 20, 1 << 20),
        )(place, mine, other, idx)

    other = swap(features)
    first, second = along(features, 1), along(other, 1)
    outgoing = pick_call("pick_features", features, (0, 0), other, (0, 0))
    first, second, outgoing, count_b = together(first, second, outgoing, count_s)
    one = jnp.concatenate([first, second])
    halo_mine = to_all(outgoing.reshape(N_DOM, HALF, f_dim))
    two, three, four, theirs_one, c_terms = together(
        along(one, 1),
        along(one, 2),
        along(first, 3),
        swap(one),
        backward(count_b),
    )
    mine = [one, two, three, four]
    theirs = [theirs_one, swap(two), swap(three), swap(four)]
    halo_mine, *theirs = together(halo_mine, *theirs)
    halo_theirs = swap(halo_mine)

    part_one = pl.pallas_call(
        pass_one_kernel,
        name="pass_one",
        out_shape=jax.ShapeDtypeStruct((4, TILE, f_dim), f32),
        in_specs=[SMEM] * 4 + [ANY] * 13,
        out_specs=VMEM,
        scratch_shapes=[
            pltpu.VMEM((COLS, TILE, f_dim), f32),
            pltpu.VMEM((COLS, 2 * TILE, f_dim), bf16),
        ]
        + tile_scr
        + [pltpu.SemaphoreType.DMA((18,))]
        + tile_sems,
        compiler_params=params(),
    )(
        place,
        rows_s,
        cols_s,
        count_s,
        *[blocks(x) for x in [features, other] + mine + theirs],
        halo_mine,
        halo_theirs,
        tiles,
    ).reshape(4 * TILE, f_dim)

    total = part_one + swap(part_one)
    low, high = total[:half_rows], total[half_rows:]
    panel = jnp.where(q == 0, total, jnp.concatenate([high, low]))
    outgoing_two = pick_call("pick_agg", panel, (0, 0), panel, (1, 0))
    one, outgoing_two = together(along(panel, 1), outgoing_two)
    fresh_mine = to_all(outgoing_two.reshape(N_DOM, HALF, f_dim))
    theirs_one = swap(one)
    early, g_early = pl.pallas_call(
        early_kernel,
        name="early",
        out_shape=(
            jax.ShapeDtypeStruct((12, 2 * TILE, h_dim), bf16),
            jax.ShapeDtypeStruct((f_dim, h_dim), f32),
        ),
        in_specs=[SMEM, VMEM, VMEM, VMEM, VMEM, ANY],
        out_specs=(VMEM, VMEM),
        scratch_shapes=[pltpu.VMEM((12, TILE, h_dim), f32), pltpu.SemaphoreType.DMA((6,))],
        compiler_params=params(),
        cost_estimate=cost(6 << 30, 4 << 20),
    )(place, blocks(panel), blocks(one), blocks(theirs_one), weight_one, c_terms)
    two, three, four, early = together(
        along(one, 1),
        along(one, 2),
        along(one[:half_rows], 3),
        early,
    )
    agg_theirs = [swap(two), swap(three), swap(four)]
    fresh_mine, *agg_theirs = together(fresh_mine, *agg_theirs)

    grads, p_keep, p_send = pl.pallas_call(
        layer_two_kernel,
        name="layer_two",
        out_shape=(
            jax.ShapeDtypeStruct(((f_dim + h_dim) // 8, 2, 8, TILE), f32),
            jax.ShapeDtypeStruct((2 * TILE, h_dim), f32),
            jax.ShapeDtypeStruct((2 * TILE, h_dim), f32),
        ),
        in_specs=[SMEM] * 4 + [ANY] * 7 + [VMEM] * 4 + [ANY] * 3,
        out_specs=(VMEM, VMEM, VMEM),
        scratch_shapes=[
            pltpu.VMEM((20, TILE, f_dim), f32),
            pltpu.VMEM((COLS, 2 * TILE, h_dim), bf16),
            pltpu.VMEM((4, TILE, h_dim), f32),
            pltpu.VMEM((f_dim, h_dim), f32),
            pltpu.VMEM((N_DOM, TILE, h_dim), f32),
            pltpu.VMEM((20, TILE, h_dim), f32),
        ]
        + tile_scr
        + [pltpu.SemaphoreType.DMA((18,))]
        + tile_sems
        + [pltpu.SemaphoreType.DMA((N_ROW,))],
        compiler_params=params(),
        cost_estimate=cost(8 << 30, 16 << 20),
    )(
        place,
        rows_s,
        cols_s,
        count_s,
        *[blocks(x) for x in [two, three, four] + agg_theirs],
        early,
        g_early,
        weight_one,
        weight_two,
        cotangent,
        blocks(history),
        c_terms,
        tiles,
    )

    fresh_mine, grads = together(fresh_mine, grads)
    fresh_theirs = swap(fresh_mine)
    output = p_keep + swap(p_send)
    part = grads.reshape(N_DOM * N_REP, -1, TILE)
    part = lax.all_to_all(part, ("dom", "rep"), split_axis=0, concat_axis=0, tiled=True)
    part = jnp.sum(part, axis=0)
    part = jnp.broadcast_to(part[None], (N_ROW,) + part.shape)
    part = lax.all_to_all(part, "row", split_axis=0, concat_axis=0, tiled=True)
    part = jnp.sum(part, axis=0)
    part, place_late = together(part, place)
    fresh = pl.pallas_call(
        fresh_kernel,
        name="fresh",
        out_shape=jax.ShapeDtypeStruct((N_DOM * TILE, h_dim), f32),
        in_specs=[SMEM, VMEM, VMEM, VMEM],
        out_specs=VMEM,
        compiler_params=params(),
        cost_estimate=cost(6 * N_DOM * TILE * f_dim * h_dim, 4 << 20),
    )(place_late, fresh_mine, fresh_theirs, weight_one)
    part = jnp.broadcast_to(part[None], (N_DOM * N_REP,) + part.shape)
    part = lax.all_to_all(part, ("dom", "rep"), split_axis=0, concat_axis=0, tiled=True)
    part, output, fresh = together(part, output, fresh)
    grads = part.reshape(-1, 2, 8, TILE).transpose(0, 2, 1, 3).reshape(-1, h_dim)
    return (output, grads[:f_dim], grads[f_dim:], fresh)


def solution(mesh):
    return jax.shard_map(
        local,
        mesh=mesh,
        in_specs=(
            P(("dom", "row", "rep"), None),
            P("dom", "row", None, None),
            P("dom", "row", "rep", None, None),
            P("dom", "row", "rep"),
            P("dom", "row", "rep"),
            P("dom", "row", "rep"),
            P(("dom", "row"), None),
            P(),
            P(),
            P(("dom", "row"), None),
        ),
        out_specs=(P(("dom", "row", "rep"), None), P(), P(), P(("dom", "row"), None)),
        check_vma=False,
    )
```

```python
import jax
import jax.numpy as jnp
from jax import lax
from jax.experimental import pallas as pl
from jax.experimental.pallas import tpu as pltpu
from jax.sharding import PartitionSpec as P

f32 = jnp.float32
bf16 = jnp.bfloat16
TILE = 128
HALF = 64
N_DOM, N_ROW, N_REP = 16, 8, 2
OWN = 32
COLS = 48
SLOTS = 64
GROUP = 8
NN = (((1,), (0,)), ((), ()))
TN = (((0,), (0,)), ((), ()))
NT = (((1,), (1,)), ((), ()))
VMEM_LIMIT = 63 * 1024 * 1024


def split2(x):
    hi = x.astype(bf16)
    lo = (x - hi.astype(f32)).astype(bf16)
    return hi, lo


def split3(x):
    hi = x.astype(bf16)
    rest = x - hi.astype(f32)
    mid = rest.astype(bf16)
    lo = (rest - mid.astype(f32)).astype(bf16)
    return hi, mid, lo


def mm(a, b, dims):
    return lax.dot_general(a, b, dims, preferred_element_type=f32)


def dot3(a, b, dims):
    a_hi, a_lo = split2(a)
    b_hi, b_lo = split2(b)
    return mm(a_hi, b_hi, dims) + (mm(a_hi, b_lo, dims) + mm(a_lo, b_hi, dims))


def pick_rows(q, panel, idx_ref, out_ref):
    rhs = jnp.concatenate(split3(panel), axis=1)
    lane = lax.broadcasted_iota(jnp.int32, (TILE, TILE), 1).astype(f32)
    for b in range(N_DOM // 2):
        cols = []
        for p in (2 * b, 2 * b + 1):
            col = jnp.broadcast_to(idx_ref[p : p + 1, :].astype(f32), (TILE, TILE)).T
            cols.append(jnp.where(q == 0, col[:HALF], col[HALF:]))
        col = jnp.concatenate(cols, axis=0)
        marks = [
            jnp.where(col == lane + float(k * TILE), 1.0, 0.0).astype(bf16)
            for k in range(panel.shape[0] // TILE)
        ]
        got = mm(jnp.concatenate(marks, axis=1), rhs, NN)
        out_ref[pl.ds(b * TILE, TILE), :] = (
            got[:, :TILE] + got[:, TILE : 2 * TILE]
        ) + got[:, 2 * TILE :]


def pick_kernel(place, mine, other, idx_ref, out_ref):
    q = place[0]
    a, b = mine[...], other[...]
    panel = jnp.concatenate([jnp.where(q == 0, a, b), jnp.where(q == 0, b, a)], axis=0)
    pick_rows(q, panel, idx_ref, out_ref)


def tile_copies(tiles_hbm, tiles, sems):
    return [
        pltpu.make_async_copy(
            tiles_hbm.at[pl.ds(k * GROUP, GROUP)], tiles.at[pl.ds(k * GROUP, GROUP)], sems.at[k]
        )
        for k in range(SLOTS // GROUP)
    ]


def each_tile(count_s, tiles_hbm, tiles, sems, one_tile):
    count = count_s[0, 0]

    def body(g, carry):
        part = pl.ds(g * GROUP, GROUP)
        pltpu.make_async_copy(tiles_hbm.at[part], tiles.at[part], sems.at[g]).wait()

        @pl.when(g * GROUP < count)
        def _():
            for i in range(GROUP):
                t = g * GROUP + i
                live = jnp.where(t < count, 1.0, 0.0).astype(f32)
                one_tile(t, tiles[t] * live)

        return carry

    lax.fori_loop(0, SLOTS // GROUP, body, 0)


def backward_kernel(rows_s, cols_s, count_s, cot, w2, tiles_hbm, out, u_scr, tiles, sems):
    for c in tile_copies(tiles_hbm, tiles, sems):
        c.start()
    out[...] = jnp.zeros_like(out)
    for b in range(4):
        hi, lo = split2(dot3(cot[pl.ds(b * TILE, TILE), :], w2[...], NT))
        u_scr[b, :TILE, :] = hi
        u_scr[b, TILE:, :] = lo

    def one_tile(t, a):
        a_hi, a_lo = split2(a)
        u = u_scr[rows_s[0, t]]
        term = mm(jnp.concatenate([a_hi, a_hi], axis=0), u, TN) + mm(a_lo, u[:TILE], TN)
        out[jnp.minimum(cols_s[0, t], OWN)] += term

    each_tile(count_s, tiles_hbm, tiles, sems, one_tile)


def forward_tiles(rows_s, cols_s, count_s, tiles_hbm, tiles, sems, x_scr, acc):
    def one_tile(t, a):
        a_hi, a_lo = split2(a)
        x = x_scr[cols_s[0, t]]
        term = mm(jnp.concatenate([a_hi, a_hi], axis=1), x, NN) + mm(a_lo, x[:TILE], NN)
        acc[rows_s[0, t]] += term

    each_tile(count_s, tiles_hbm, tiles, sems, one_tile)


def piece_copies(place, own, mine, theirs, dst, sems):
    q, r = place[0], place[1]
    side = 1 - 2 * q
    parts = [(own[0], r, q), (own[1], r, 1 - q)]
    for refs, way, half in ((mine, side, q), (theirs, -side, 1 - q)):
        for s in (1, 2, 3):
            row = lax.rem(r + N_ROW - way * s, N_ROW)
            parts.append((refs[s - 1].at[pl.ds(0, 2)], row, half))
            parts.append((refs[s - 1].at[pl.ds(2, 2)], row, 1 - half))
        parts.append((refs[3], lax.rem(r + 4, N_ROW), half))
    return [
        pltpu.make_async_copy(ref, dst.at[pl.ds(row * 4 + half * 2, 2)], sems.at[k])
        for k, (ref, row, half) in enumerate(parts)
    ]


def pass_one_kernel(place, rows_s, cols_s, count_s, *refs):
    own, other, mine, theirs = refs[0], refs[1], refs[2:6], refs[6:10]
    halo_mine, halo_theirs, tiles_hbm, acc, xf, x_scr, tiles, sems, tile_sems = refs[10:]
    q = place[0]
    copies = piece_copies(place, (own, other), mine, theirs, xf, sems)
    for m, (ref, half) in enumerate(((halo_mine, q), (halo_theirs, 1 - q))):
        at = pl.multiple_of(half * HALF, HALF)
        copies.append(
            pltpu.make_async_copy(
                ref, xf.at[pl.ds(OWN, N_DOM), pl.ds(at, HALF), :], sems.at[16 + m]
            )
        )
    for c in copies + tile_copies(tiles_hbm, tiles, tile_sems):
        c.start()
    acc[...] = jnp.zeros_like(acc)
    for c in copies:
        c.wait()

    def body(j, carry):
        for k in range(4):
            hi, lo = split2(xf[j * 4 + k])
            x_scr[j * 4 + k, :TILE, :] = hi
            x_scr[j * 4 + k, TILE:, :] = lo
        return carry

    lax.fori_loop(0, COLS // 4, body, 0)
    forward_tiles(rows_s, cols_s, count_s, tiles_hbm, tiles, tile_sems, x_scr, acc)


def hidden_step(x, terms, w_hi, w_lo, h_ref, at, n):
    total = jnp.zeros((TILE, w_hi.shape[1]), f32)
    for b in range(n):
        x_b = x[b]
        x_hi, x_lo = split2(x_b)
        pre = mm(x_hi, w_hi, NN) + (mm(x_hi, w_lo, NN) + mm(x_lo, w_hi, NN))
        sig = 1.0 / (1.0 + jnp.exp(-pre))
        hi, lo = split2(pre * sig)
        h_ref[at + b, :TILE, :] = hi
        h_ref[at + b, TILE:, :] = lo
        grad = terms[b] * (sig * (1.0 + pre * (1.0 - sig)))
        total += dot3(x_b, grad, TN)
    return total


def early_kernel(place, own, one, their_one, w1, c_hbm, hidden, g_out, c_terms, sems):
    q, r = place[0], place[1]
    side = 1 - 2 * q
    copies = []
    for k, (row, half) in enumerate(early_parts(r, q, side)):
        for h in (0, 1):
            at = row * 4 + 2 * (half if h == 0 else 1 - half)
            copies.append(
                pltpu.make_async_copy(
                    c_hbm.at[pl.ds(at, 2)], c_terms.at[pl.ds(4 * k + 2 * h, 2)], sems.at[2 * k + h]
                )
            )
    for c in copies:
        c.start()
    w_hi, w_lo = split2(w1[...])
    total = jnp.zeros(g_out.shape, f32)
    for k, x in enumerate((own, one, their_one)):
        copies[2 * k].wait()
        copies[2 * k + 1].wait()
        total += hidden_step(x, c_terms.at[pl.ds(4 * k, 4)], w_hi, w_lo, hidden, 4 * k, 4)
    g_out[...] = total


def early_parts(r, q, side):
    below = lax.rem(r + N_ROW - side, N_ROW)
    above = lax.rem(r + N_ROW + side, N_ROW)
    return ((r, q), (below, q), (above, 1 - q))


def layer_two_kernel(place, rows_s, cols_s, count_s, *refs):
    mine, theirs = refs[0:3], refs[3:6]
    (early, g_early, w1, w2, cot, hist_hbm, c_hbm, tiles_hbm) = refs[6:14]
    grads, p_keep, p_send = refs[14:17]
    (xf, h_scr, acc, g_one, hist, c_terms, tiles, sems, tile_sems, c_sems) = refs[17:]
    q, r = place[0], place[1]
    side = 1 - 2 * q
    parts = []
    for refs_m, way, half in ((mine, side, q), (theirs, -side, 1 - q)):
        for n, s in ((0, 2), (1, 3)):
            slot = lax.rem(2 * N_ROW - way * s, N_ROW) - 2
            parts.append((refs_m[n].at[pl.ds(0, 2)], slot, half))
            parts.append((refs_m[n].at[pl.ds(2, 2)], slot, 1 - half))
        parts.append((refs_m[2], 2, half))
    copies = [
        pltpu.make_async_copy(ref, xf.at[pl.ds(slot * 4 + half * 2, 2)], sems.at[k])
        for k, (ref, slot, half) in enumerate(parts)
    ]
    late = []
    for k, (row, half) in enumerate(early_parts(r, q, side)):
        for h in (0, 1):
            at = row * 4 + 2 * (half if h == 0 else 1 - half)
            late.append(
                pltpu.make_async_copy(
                    early.at[pl.ds(4 * k + 2 * h, 2)], h_scr.at[pl.ds(at, 2)], sems.at[10 + 2 * k + h]
                )
            )
    late.append(pltpu.make_async_copy(hist_hbm, hist, sems.at[16]))

    def row_of(g):
        return lax.rem(r + 2 + g, N_ROW)

    def c_copy(g):
        return pltpu.make_async_copy(
            c_hbm.at[pl.ds(row_of(g) * 4, 4)], c_terms.at[pl.ds(g * 4, 4)], c_sems.at[g]
        )

    for c in copies:
        c.start()
    for g in range(5):
        c_copy(g).start()
    for c in late + tile_copies(tiles_hbm, tiles, tile_sems):
        c.start()
    acc[...] = jnp.zeros_like(acc)
    g_one[...] = g_early[...]
    w_hi, w_lo = split2(w1[...])
    for c in copies:
        c.wait()

    def panel_step(g, carry):
        c_copy(g).wait()
        part = pl.ds(g * 4, 4)
        g_one[...] += hidden_step(xf.at[part], c_terms.at[part], w_hi, w_lo, h_scr, row_of(g) * 4, 4)
        return carry

    lax.fori_loop(0, 5, panel_step, 0)
    for c in late:
        c.wait()

    def hist_step(g, carry):
        for b in range(2):
            hi, lo = split2(hist[g * 2 + b])
            h_scr[OWN + g * 2 + b, :TILE, :] = hi
            h_scr[OWN + g * 2 + b, TILE:, :] = lo
        return carry

    lax.fori_loop(0, N_DOM // 2, hist_step, 0)
    forward_tiles(rows_s, cols_s, count_s, tiles_hbm, tiles, tile_sems, h_scr, acc)

    agg = acc[...].reshape(4 * TILE, -1)
    g_two = dot3(agg, cot[...], TN)
    for h in (0, 1):
        cols = pl.ds(h * TILE, TILE)
        grads[: g_one.shape[0] // 8, h] = g_one[:, cols].reshape(-1, 8, TILE)
        grads[g_one.shape[0] // 8 :, h] = g_two[:, h * TILE : (h + 1) * TILE].reshape(-1, 8, TILE)
    prod = dot3(agg, w2[...], NN)
    low, high = prod[: 2 * TILE], prod[2 * TILE :]
    p_keep[...] = jnp.where(q == 0, low, high)
    p_send[...] = jnp.where(q == 0, high, low)


def fresh_kernel(place, mine, theirs, w1, out):
    q = place[0]
    w_hi, w_lo = split2(w1[...])
    for s in range(mine.shape[0]):
        a, b = mine[s], theirs[s]
        x = jnp.concatenate([jnp.where(q == 0, a, b), jnp.where(q == 0, b, a)], axis=0)
        x_hi, x_lo = split2(x)
        pre = mm(x_hi, w_hi, NN) + (mm(x_hi, w_lo, NN) + mm(x_lo, w_hi, NN))
        out[pl.ds(s * TILE, TILE), :] = pre / (1.0 + jnp.exp(-pre))


SMEM = pl.BlockSpec(memory_space=pltpu.SMEM)
VMEM = pl.BlockSpec(memory_space=pltpu.VMEM)
ANY = pl.BlockSpec(memory_space=pltpu.HBM)


def params():
    return pltpu.CompilerParams(vmem_limit_bytes=VMEM_LIMIT)


def cost(flops, moved):
    return pl.CostEstimate(flops=flops, bytes_accessed=moved, transcendentals=0)


def swap(x):
    return lax.ppermute(x, "rep", [(0, 1), (1, 0)])


def along(x, k):
    pairs = []
    for row in range(N_ROW):
        for core in range(N_REP):
            to = row - k if core else row + k
            pairs.append((row * N_REP + core, to % N_ROW * N_REP + core))
    return lax.ppermute(x, ("row", "rep"), pairs)


def together(*xs):
    return lax.optimization_barrier(xs)


def blocks(x):
    return x.reshape(-1, TILE, x.shape[-1])


def to_all(x):
    return lax.all_to_all(x, "dom", split_axis=0, concat_axis=0, tiled=True)


def local(
    features,
    send_rows,
    tile_values,
    tile_rows,
    tile_cols,
    tile_counts,
    history,
    weight_one,
    weight_two,
    cotangent,
):
    f_dim, h_dim = weight_one.shape
    half_rows = features.shape[0]
    tiles = tile_values.reshape(SLOTS, TILE, TILE)
    rows_s = tile_rows.reshape(1, SLOTS)
    cols_s = tile_cols.reshape(1, SLOTS)
    count_s = tile_counts.reshape(1, 1)
    idx = send_rows.reshape(N_DOM, TILE)
    q = lax.axis_index("rep")
    place = jnp.stack([q, lax.axis_index("row")]).astype(jnp.int32)
    tile_scr = [pltpu.VMEM((SLOTS, TILE, TILE), f32)]
    tile_sems = [pltpu.SemaphoreType.DMA((SLOTS // GROUP,))]

    def backward(count_s):
        return pl.pallas_call(
            backward_kernel,
            name="backward",
            out_shape=jax.ShapeDtypeStruct((OWN + 1, TILE, h_dim), f32),
            in_specs=[SMEM, SMEM, SMEM, VMEM, VMEM, ANY],
            out_specs=VMEM,
            scratch_shapes=[pltpu.VMEM((4, 2 * TILE, h_dim), bf16)] + tile_scr + tile_sems,
            compiler_params=params(),
            cost_estimate=cost(6 * SLOTS * TILE * TILE * h_dim, 9 << 20),
        )(rows_s, cols_s, count_s, cotangent, weight_two, tiles)

    def pick_call(name, mine, mine_at, other, other_at):
        return pl.pallas_call(
            pick_kernel,
            name=name,
            grid=(1,),
            out_shape=jax.ShapeDtypeStruct((N_DOM * HALF, f_dim), f32),
            in_specs=[
                SMEM,
                pl.BlockSpec((half_rows, f_dim), lambda g: mine_at),
                pl.BlockSpec((half_rows, f_dim), lambda g: other_at),
                VMEM,
            ],
            out_specs=VMEM,
            compiler_params=params(),
            cost_estimate=cost(1 << 20, 1 << 20),
        )(place, mine, other, idx)

    other = swap(features)
    first, second = along(features, 1), along(other, 1)
    outgoing = pick_call("pick_features", features, (0, 0), other, (0, 0))
    first, second, outgoing, count_b = together(first, second, outgoing, count_s)
    one = jnp.concatenate([first, second])
    halo_mine = to_all(outgoing.reshape(N_DOM, HALF, f_dim))
    two, three, four, theirs_one, c_terms = together(
        along(one, 1),
        along(one, 2),
        along(first, 3),
        swap(one),
        backward(count_b),
    )
    mine = [one, two, three, four]
    theirs = [theirs_one, swap(two), swap(three), swap(four)]
    halo_mine, *theirs = together(halo_mine, *theirs)
    halo_theirs = swap(halo_mine)

    part_one = pl.pallas_call(
        pass_one_kernel,
        name="pass_one",
        out_shape=jax.ShapeDtypeStruct((4, TILE, f_dim), f32),
        in_specs=[SMEM] * 4 + [ANY] * 13,
        out_specs=VMEM,
        scratch_shapes=[
            pltpu.VMEM((COLS, TILE, f_dim), f32),
            pltpu.VMEM((COLS, 2 * TILE, f_dim), bf16),
        ]
        + tile_scr
        + [pltpu.SemaphoreType.DMA((18,))]
        + tile_sems,
        compiler_params=params(),
    )(
        place,
        rows_s,
        cols_s,
        count_s,
        *[blocks(x) for x in [features, other] + mine + theirs],
        halo_mine,
        halo_theirs,
        tiles,
    ).reshape(4 * TILE, f_dim)

    total = part_one + swap(part_one)
    low, high = total[:half_rows], total[half_rows:]
    panel = jnp.where(q == 0, total, jnp.concatenate([high, low]))
    outgoing_two = pick_call("pick_agg", panel, (0, 0), panel, (1, 0))
    one, outgoing_two = together(along(panel, 1), outgoing_two)
    theirs_one, outgoing_two = together(swap(one), outgoing_two)
    fresh_mine = to_all(outgoing_two.reshape(N_DOM, HALF, f_dim))
    early, g_early = pl.pallas_call(
        early_kernel,
        name="early",
        out_shape=(
            jax.ShapeDtypeStruct((12, 2 * TILE, h_dim), bf16),
            jax.ShapeDtypeStruct((f_dim, h_dim), f32),
        ),
        in_specs=[SMEM, VMEM, VMEM, VMEM, VMEM, ANY],
        out_specs=(VMEM, VMEM),
        scratch_shapes=[pltpu.VMEM((12, TILE, h_dim), f32), pltpu.SemaphoreType.DMA((6,))],
        compiler_params=params(),
        cost_estimate=cost(6 << 30, 4 << 20),
    )(place, blocks(panel), blocks(one), blocks(theirs_one), weight_one, c_terms)
    two, three, four, early = together(
        along(one, 1),
        along(one, 2),
        along(one[:half_rows], 3),
        early,
    )
    agg_theirs = [swap(two), swap(three), swap(four)]
    fresh_mine, *agg_theirs = together(fresh_mine, *agg_theirs)

    grads, p_keep, p_send = pl.pallas_call(
        layer_two_kernel,
        name="layer_two",
        out_shape=(
            jax.ShapeDtypeStruct(((f_dim + h_dim) // 8, 2, 8, TILE), f32),
            jax.ShapeDtypeStruct((2 * TILE, h_dim), f32),
            jax.ShapeDtypeStruct((2 * TILE, h_dim), f32),
        ),
        in_specs=[SMEM] * 4 + [ANY] * 7 + [VMEM] * 4 + [ANY] * 3,
        out_specs=(VMEM, VMEM, VMEM),
        scratch_shapes=[
            pltpu.VMEM((20, TILE, f_dim), f32),
            pltpu.VMEM((COLS, 2 * TILE, h_dim), bf16),
            pltpu.VMEM((4, TILE, h_dim), f32),
            pltpu.VMEM((f_dim, h_dim), f32),
            pltpu.VMEM((N_DOM, TILE, h_dim), f32),
            pltpu.VMEM((20, TILE, h_dim), f32),
        ]
        + tile_scr
        + [pltpu.SemaphoreType.DMA((18,))]
        + tile_sems
        + [pltpu.SemaphoreType.DMA((N_ROW,))],
        compiler_params=params(),
        cost_estimate=cost(8 << 30, 16 << 20),
    )(
        place,
        rows_s,
        cols_s,
        count_s,
        *[blocks(x) for x in [two, three, four] + agg_theirs],
        early,
        g_early,
        weight_one,
        weight_two,
        cotangent,
        blocks(history),
        c_terms,
        tiles,
    )

    fresh_mine, grads = together(fresh_mine, grads)
    fresh_theirs = swap(fresh_mine)
    output = p_keep + swap(p_send)
    part = grads.reshape(N_DOM * N_REP, -1, TILE)
    part = lax.all_to_all(part, ("dom", "rep"), split_axis=0, concat_axis=0, tiled=True)
    part = jnp.sum(part, axis=0)
    part = jnp.broadcast_to(part[None], (N_ROW,) + part.shape)
    part = lax.all_to_all(part, "row", split_axis=0, concat_axis=0, tiled=True)
    part = jnp.sum(part, axis=0)
    part, place_late = together(part, place)
    fresh = pl.pallas_call(
        fresh_kernel,
        name="fresh",
        out_shape=jax.ShapeDtypeStruct((N_DOM * TILE, h_dim), f32),
        in_specs=[SMEM, VMEM, VMEM, VMEM],
        out_specs=VMEM,
        compiler_params=params(),
        cost_estimate=cost(6 * N_DOM * TILE * f_dim * h_dim, 4 << 20),
    )(place_late, fresh_mine, fresh_theirs, weight_one)
    part = jnp.broadcast_to(part[None], (N_DOM * N_REP,) + part.shape)
    part = lax.all_to_all(part, ("dom", "rep"), split_axis=0, concat_axis=0, tiled=True)
    part, output, fresh = together(part, output, fresh)
    grads = part.reshape(-1, 2, 8, TILE).transpose(0, 2, 1, 3).reshape(-1, h_dim)
    return (output, grads[:f_dim], grads[f_dim:], fresh)


def solution(mesh):
    return jax.shard_map(
        local,
        mesh=mesh,
        in_specs=(
            P(("dom", "row", "rep"), None),
            P("dom", "row", None, None),
            P("dom", "row", "rep", None, None),
            P("dom", "row", "rep"),
            P("dom", "row", "rep"),
            P("dom", "row", "rep"),
            P(("dom", "row"), None),
            P(),
            P(),
            P(("dom", "row"), None),
        ),
        out_specs=(P(("dom", "row", "rep"), None), P(), P(), P(("dom", "row"), None)),
        check_vma=False,
    )
```
